32 devices in a mesh: groups: 2 (over x), wide: 16 (over z, y, core).
Axes of the slice: x: 2, y: 2, z: 4, core: 2. Of those that a mesh axis runs over, the one named last changes fastest.
Arguments:
- loader_features: bfloat16 [32768, 128], P(('groups', 'wide')), parts along dimension 0, may hold values from -6 to 6
- dest: int32 [32768], P(('groups', 'wide')), parts along dimension 0, may hold values from 0 to 16383, as said below
- block_values: bfloat16 [8192, 128, 128], P(('groups', 'wide')), parts along dimension 0, may hold values from -0.09375 to 0.09375
- row_block: int32 [8192], P(('groups', 'wide')), parts along dimension 0, may hold values from 0 to 7, as said below
- col_block: int32 [8192], P(('groups', 'wide')), parts along dimension 0, may hold values from 0 to 127, as said below
- w_first: bfloat16 [128, 256], replicated, may hold values from -0.5 to 0.5
- b_first: float32 [256], replicated, may hold values from -3 to 3
- w_second: bfloat16 [256, 256], replicated, may hold values from -0.375 to 0.375
- b_second: float32 [256], replicated, may hold values from -3 to 3
Outputs:
- output: bfloat16 [32768, 256], P(('groups', 'wide')), parts along dimension 0
The draws below stay inside these ranges and needn't reach their ends.
There are 2 independent parts, one for each index of `groups`. The reference program is written for one: setup_inputs(seed, part) draws one part's arguments, and reference() takes and returns one part's arrays. A program takes and returns all parts, laid end to end along the dimension named above; an argument that names none is the same for every part. Nothing has to cross between parts.
Inputs may be any that keep to these rules, and one draw needn't show every extreme that they name: dest is a permutation; row i goes to owner dest[i] // 1024. Each device sends at most 256 of its rows to one owner and exactly 256 to some owner; every owner receives exactly 256 rows from some device. `col_block`: A device's list holds 16 groups of 16 entries; in group g every column block lies in device g's nodes (g * 8 to g * 8 + 7); the k-th entry's column block depends only on k mod 2, and these 2 are distinct. `row_block`: in each group, the k-th entry's row block is distinct among entries with the same k mod 2.
All inputs are finite; a program needn't handle non-finite values.
Results may differ from the reference program's by a relative error of at most 0.0058.
Values may be sent and summed in bfloat16 or wider, within the bound.
A program may use at most 128 MiB of HBM per device.

```python
import jax
import jax.numpy as jnp
from jax import lax

F = 128
HID = 256
BLK = 128
USED = 2
NODE_DEV = 1024
RB = 8
SLOTS = 16
CAP = 256
NODES = 16384
N_WIDE = 16


def block_pattern(key):
    key_cols = jax.random.fold_in(key, 11)
    key_rows = jax.random.fold_in(key, 12)
    group_count = N_WIDE * N_WIDE
    col_perm = jax.vmap(lambda sub: jax.random.permutation(sub, RB))(jax.random.split(key_cols, group_count))[:, :USED]
    row_perm = jax.vmap(lambda sub: jax.random.permutation(sub, RB))(jax.random.split(key_rows, group_count * USED))
    row_perm = row_perm.reshape(group_count, USED, RB)
    rows = jnp.transpose(row_perm, (0, 2, 1)).reshape(group_count * SLOTS)
    source = jnp.arange(group_count, dtype=jnp.int32) % N_WIDE
    cols = source[:, None, None] * RB + col_perm[:, None, :]
    cols = jnp.broadcast_to(cols, (group_count, RB, USED)).reshape(group_count * SLOTS)
    return (rows.astype(jnp.int32), cols.astype(jnp.int32))


def draw_row_block(key, part):
    return block_pattern(key)[0]


def draw_col_block(key, part):
    return block_pattern(key)[1]


def draw_dest(key, part):
    count = N_WIDE
    rest = NODE_DEV - CAP
    share = rest // (count - 1)
    extra = rest % (count - 1)
    base = share + (jnp.arange(count - 1) < extra).astype(jnp.int32)
    half = (count - 1) // 2
    swing = jax.random.randint(jax.random.fold_in(key, 21), (half,), -(share // 2), share // 2 + 1)
    delta = jnp.zeros((count - 1,), jnp.int32).at[:half].set(swing).at[half:2 * half].add(-swing)
    spread = jax.random.permutation(jax.random.fold_in(key, 22), base + delta)
    weights = jnp.concatenate([jnp.full((1,), CAP, jnp.int32), spread.astype(jnp.int32)])
    sigma = jax.random.permutation(jax.random.fold_in(key, 23), count)
    tau = jax.random.permutation(jax.random.fold_in(key, 24), count)
    counts = weights[(sigma[None, :] - tau[:, None]) % count]
    row_cum = jnp.cumsum(counts, axis=1)
    row_excl = row_cum - counts
    col_excl = jnp.cumsum(counts, axis=0) - counts
    position = jnp.arange(NODE_DEV, dtype=jnp.int32)
    owner = jax.vmap(lambda cum: jnp.searchsorted(cum, position, side='right'))(row_cum).astype(jnp.int32)
    slot = jnp.take_along_axis(col_excl, owner, axis=1) + position[None, :] - jnp.take_along_axis(row_excl, owner, axis=1)
    owner_perm = jax.vmap(lambda sub: jax.random.permutation(sub, NODE_DEV))(jax.random.split(jax.random.fold_in(key, 25), count))
    final = owner * NODE_DEV + owner_perm[owner, slot]
    source_perm = jax.vmap(lambda sub: jax.random.permutation(sub, NODE_DEV))(jax.random.split(jax.random.fold_in(key, 26), count))
    placed = jnp.zeros((count, NODE_DEV), jnp.int32).at[jnp.arange(count)[:, None], source_perm].set(final)
    return placed.reshape(count * NODE_DEV).astype(jnp.int32)


def block_levels(rng, extent, cuts, least, largest):
    level, own = 1.0, jax.random.fold_in(rng, 6)
    for axis_at, parts in cuts:
        steps = jnp.exp(jax.random.uniform(jax.random.fold_in(own, axis_at), (parts,), jnp.float32, least / len(cuts), largest / len(cuts)))
        level = level * jnp.repeat(steps, extent[axis_at] // parts).reshape([-1 if axis == axis_at else 1 for axis in range(len(extent))])
    return level


def noise(rng, shape, scale, bound, cuts=(), held_as=jnp.bfloat16):
    result = jax.random.normal(rng, shape, jnp.float32) * scale
    if len(cuts) > 0:
        result = block_levels(rng, shape, cuts, -0.22, 0.18) * result
    return jnp.clip(result, min=-bound, max=bound).astype(held_as)


def setup_inputs(seed: int = 0, part: int = 0) -> dict:
    arg_keys = jax.random.split(jax.random.key(seed), 10)
    part_keys = jax.random.split(jax.random.fold_in(arg_keys[9], part), 10)
    loader_features = noise(part_keys[0], (NODES, F), 1.0, 6.0, ((0, 16),))
    dest = draw_dest(jax.random.fold_in(jax.random.fold_in(arg_keys[9], part), 71), part)
    block_values = noise(part_keys[2], (N_WIDE * N_WIDE * SLOTS, BLK, BLK), (N_WIDE * USED * BLK) ** -0.5, 0.09375, ((0, 16),))
    row_block = draw_row_block(jax.random.fold_in(jax.random.fold_in(arg_keys[9], part), 71), part)
    col_block = draw_col_block(jax.random.fold_in(jax.random.fold_in(arg_keys[9], part), 71), part)
    w_first = noise(arg_keys[5], (F, HID), F ** -0.5, 0.5)
    b_first = noise(arg_keys[6], (HID,), 0.5, 3.0, (), jnp.float32)
    w_second = noise(arg_keys[7], (HID, HID), HID ** -0.5, 0.375)
    b_second = noise(arg_keys[8], (HID,), 0.5, 3.0, (), jnp.float32)
    return dict(loader_features=loader_features, dest=dest, block_values=block_values, row_block=row_block, col_block=col_block, w_first=w_first, b_first=b_first, w_second=w_second, b_second=b_second)


def aggregate(panel, block_values, row_block, col_block):
    width = panel.shape[1]
    tiles = panel.reshape(NODES // BLK, BLK, width)
    values = block_values.reshape(N_WIDE, N_WIDE * SLOTS, BLK, BLK)
    rows = row_block.reshape(N_WIDE, N_WIDE * SLOTS)
    cols = col_block.reshape(N_WIDE, N_WIDE * SLOTS)

    def one_owner(items):
        owned_values, owned_rows, owned_cols = items
        picked = tiles[owned_cols].astype(jnp.float32)
        products = jnp.einsum("kij,kjw->kiw", owned_values.astype(jnp.float32), picked, precision=lax.Precision.HIGHEST)
        return jax.ops.segment_sum(products, owned_rows, num_segments=RB)

    summed = lax.map(one_owner, (values, rows, cols))
    return summed.reshape(NODES, width)


def reference(loader_features, dest, block_values, row_block, col_block, w_first, b_first, w_second, b_second):
    features = jnp.zeros_like(loader_features).at[dest].set(loader_features)
    first = aggregate(features, block_values, row_block, col_block).astype(jnp.bfloat16)
    hidden = jax.nn.relu(jnp.dot(first, w_first, preferred_element_type=jnp.float32) + b_first).astype(jnp.bfloat16)
    second = aggregate(hidden, block_values, row_block, col_block).astype(jnp.bfloat16)
    output = jnp.dot(second, w_second, preferred_element_type=jnp.float32) + b_second
    return output.astype(jnp.bfloat16)
```

```python
import functools

import jax
import jax.numpy as jnp
from jax import lax
from jax.experimental import pallas as pl
from jax.experimental.pallas import tpu as pltpu
from jax.sharding import PartitionSpec as P

MESH = pl.DeviceIdType.MESH
F32 = jnp.float32
BF16 = jnp.bfloat16
I32 = jnp.int32


def greet_all(n):
    me = lax.axis_index("wide")
    barrier = pltpu.get_barrier_semaphore()

    def greet(step, _):
        pl.semaphore_signal(
            barrier, inc=1, device_id={"wide": (me + step) % n}, device_id_type=MESH
        )
        return _

    lax.fori_loop(1, n, greet, 0)
    pl.semaphore_wait(barrier, n - 1)


def gather(depth, side, buf, own_ref, sems, extra, process):
    line_send, side_send, pair_send, recv = sems
    me = lax.axis_index("wide")
    core = me % 2
    lane_y = (me // 2) % side
    lane_z = me // (2 * side)
    pair = me + 1 - 2 * core

    def slot_of(at_z, at_y, at_core):
        return (at_z * side + at_y) * 2 + at_core

    def copy(source_ref, slot, send, target):
        return pltpu.make_async_remote_copy(
            src_ref=source_ref,
            dst_ref=buf.at[slot],
            send_sem=send,
            recv_sem=recv.at[slot],
            device_id={"wide": target},
            device_id_type=MESH,
        )

    def arrived(slot):
        copy(buf.at[slot], slot, pair_send.at[0, 0], pair).wait_recv()

    def place(d):
        off = (d + 1) // 2
        at_z = lane_z + off * (1 - 2 * (d % 2))
        valid = (d >= 0) & (at_z >= 0) & (at_z < depth)
        return at_z, valid

    right = slot_of(lane_z + 1, lane_y, core)
    left = slot_of(lane_z - 1, lane_y, core)
    across = slot_of(lane_z, 1 - lane_y, core)
    steps = 2 * depth - 1
    buf[me] = own_ref[...]

    def line_copies(d, slot):
        source = buf.at[slot]
        return (
            (copy(source, slot, line_send.at[0, d], right),
             ((d == 0) | (d % 2 == 1)) & (lane_z < depth - 1)),
            (copy(source, slot, line_send.at[1, d], left),
             (d % 2 == 0) & (lane_z > 0)),
        )

    def step(d, _):
        at_z, valid = place(d)

        @pl.when(valid & (d < steps))
        def _line():
            slot = slot_of(at_z, lane_y, core)

            @pl.when(d > 0)
            def _wait():
                arrived(slot)

            for one, go in line_copies(d, slot):
                pl.when(go)(one.start)
            if side == 2:
                copy(buf.at[slot], slot, side_send.at[d], across).start()
            copy(buf.at[slot], slot, pair_send.at[0, d], pair).start()

        extra(d)

        back_z, back_valid = place(d - 2)
        if side == 2:

            @pl.when(back_valid & (d - 2 < steps))
            def _side():
                slot = slot_of(back_z, 1 - lane_y, core)
                arrived(slot)
                copy(buf.at[slot], slot, pair_send.at[1, d - 2], pair).start()

        def kind(k, _):
            lag = jnp.where(k == 0, 0, jnp.where(k == 3, 4, 2))
            from_side = k % 2
            from_pair = k // 2
            kz, kvalid = place(d - lag)
            ky = jnp.where(from_side == 1, side - 1 - lane_y, lane_y)
            kc = jnp.where(from_pair == 1, 1 - core, core)
            slot = slot_of(kz, ky, kc)

            @pl.when(kvalid & (d - lag < steps))
            def _process():
                @pl.when(from_pair == 1)
                def _wait():
                    arrived(slot)

                process(slot)

            return _

        if side == 2:
            lax.fori_loop(0, 4, kind, 0)
        else:
            lax.fori_loop(0, 2, lambda k, c: kind(2 * k, c), 0)
        return _

    lax.fori_loop(0, steps + 4, step, 0)

    def drain(d, _):
        at_z, valid = place(d)

        @pl.when(valid)
        def _drain():
            slot = slot_of(at_z, lane_y, core)
            for one, go in line_copies(d, slot):
                pl.when(go)(one.wait_send)
            if side == 2:
                copy(buf.at[slot], slot, side_send.at[d], across).wait_send()
                other = slot_of(at_z, 1 - lane_y, core)
                copy(buf.at[other], other, pair_send.at[1, d], pair).wait_send()
            copy(buf.at[slot], slot, pair_send.at[0, d], pair).wait_send()

        return _

    lax.fori_loop(0, steps, drain, 0)


def rows_kernel(
    depth, side, dest_ref, loader_ref, table, inverse_int,
    rows_buf, dest_buf, inverse, dest_send, dest_recv, *sems
):
    n = depth * side * 2
    node_dev = loader_ref.shape[0]
    block = dest_ref.shape[1]
    row_blocks = node_dev // block
    me = lax.axis_index("wide")
    greet_all(n)

    def dest_copy(step, source):
        return pltpu.make_async_remote_copy(
            src_ref=dest_ref,
            dst_ref=dest_buf.at[source],
            send_sem=dest_send.at[step],
            recv_sem=dest_recv.at[source],
            device_id={"wide": (me + step) % n},
            device_id_type=MESH,
        )

    def send_dest(step, _):
        dest_copy(step, me).start()
        return _

    lax.fori_loop(1, n, send_dest, 0)
    dest_buf[me] = dest_ref[...]
    inverse[...] = jnp.zeros_like(inverse)

    blocks = n * row_blocks
    sub_hi = lax.broadcasted_iota(I32, (blocks, block), 0)
    sub_lo = lax.broadcasted_iota(I32, (block, block), 0)
    lane_hi = lax.broadcasted_iota(I32, (blocks, block), 1).astype(F32)

    def invert(source):
        @pl.when(source != me)
        def _wait():
            dest_copy(1, source).wait_recv()

        positions = dest_buf[source]
        upper, lower, right = [], [], []
        for a in range(row_blocks):
            line = positions[a : a + 1, :]
            hit = sub_hi == line // block
            number = (source * row_blocks + a).astype(F32)
            upper.append(jnp.where(hit, number, 0.0).astype(BF16))
            lower.append(jnp.where(hit, lane_hi, 0.0).astype(BF16))
            right.append(jnp.where(sub_lo == line % block, 1.0, 0.0).astype(BF16))
        left = jnp.concatenate(
            [jnp.concatenate(upper, axis=1), jnp.concatenate(lower, axis=1)], axis=0
        )
        inverse[...] += lax.dot_general(
            left,
            jnp.concatenate(right, axis=1),
            (((1,), (1,)), ((), ())),
            preferred_element_type=F32,
        )

    def invert_two(d):
        def one(k, _):
            source = 2 * d + k
            pl.when(source < n)(lambda: invert(source))
            return _

        lax.fori_loop(0, 2, one, 0)

    def widen(slot):
        start = pl.multiple_of(slot * node_dev, node_dev)
        table[pl.ds(start, node_dev), :] = rows_buf[slot].astype(F32)

    gather(depth, side, rows_buf, loader_ref, sems, invert_two, widen)

    def drain_dest(step, _):
        dest_copy(step, me).wait_send()
        return _

    lax.fori_loop(1, n, drain_dest, 0)

    inverse_int[...] = (
        inverse[:blocks, :] * float(block) + inverse[blocks:, :]
    ).astype(I32)


def add(group, right, values, total, row_blocks):
    block = values.shape[1]
    for r in range(row_blocks):
        at = (group * row_blocks + r) * 2
        left = jnp.concatenate([values[at], values[at + 1]], axis=1)
        total[pl.ds(r * block, block), :] += jnp.dot(
            left, right, preferred_element_type=F32
        )


def first_kernel(
    n, col_ref, order_ref, inverse_ref, table_ref, values_ref, first_ref, ordered_ref,
    values, picked, total, local_sem
):
    def load_block(at, _):
        pltpu.make_async_copy(
            values_ref.at[order_ref[at]], values.at[at], local_sem.at[0]
        ).start()
        return _

    lax.fori_loop(0, values.shape[0], load_block, 0, unroll=8)
    block = values.shape[1]
    row_blocks = first_ref.shape[0] // block
    slots = values.shape[0] // n

    def pick(t, _):
        column = col_ref[(t // 2) * slots + t % 2]

        def fetch(j, _):
            for k in range(16):
                row = inverse_ref[column, j * 16 + k]
                picked[pl.ds(t * block + j * 16 + k, 1), :] = table_ref[pl.ds(row, 1), :]
            return _

        return lax.fori_loop(0, block // 16, fetch, _)

    lax.fori_loop(0, 2 * n, pick, 0)
    pltpu.make_async_copy(values_ref, values, local_sem.at[0]).wait()
    store = pltpu.make_async_copy(values, ordered_ref, local_sem.at[1])
    store.start()
    total[...] = jnp.zeros_like(total)

    def group_step(group, _):
        start = pl.multiple_of(group * 2 * block, 2 * block)
        right = picked[pl.ds(start, 2 * block), :].astype(BF16)
        add(group, right, values, total, row_blocks)
        return _

    lax.fori_loop(0, n, group_step, 0)
    first_ref[...] = total[...].astype(BF16)
    store.wait()


def second_kernel(
    depth, side, col_ref, first_ref, values_ref,
    w_first_ref, b_first_ref, w_second_ref, b_second_ref, out_ref,
    values, first_buf, total, local_sem, *sems
):
    n = depth * side * 2
    load = pltpu.make_async_copy(values_ref, values, local_sem)
    load.start()
    block = values.shape[1]
    row_blocks = first_ref.shape[0] // block
    slots = values.shape[0] // n
    greet_all(n)
    total[...] = jnp.zeros_like(total)
    load.wait()

    def second_group(slot):
        tiles = []
        for u in range(2):
            column = col_ref[slot * slots + u] - slot * row_blocks
            tile = first_buf[slot, :block]
            for b in range(1, row_blocks):
                tile = jnp.where(
                    column == b, first_buf[slot, b * block : (b + 1) * block], tile
                )
            tiles.append(tile)
        tiles = jnp.concatenate(tiles, axis=0)
        hidden = jnp.dot(tiles, w_first_ref[...], preferred_element_type=F32)
        hidden = jnp.maximum(hidden + b_first_ref[...], 0.0).astype(BF16)
        add(slot, hidden, values, total, row_blocks)

    gather(depth, side, first_buf, first_ref, sems, lambda d: None, second_group)
    out_ref[...] = (
        jnp.dot(total[...].astype(BF16), w_second_ref[...], preferred_element_type=F32)
        + b_second_ref[...]
    ).astype(BF16)


def body(
    depth, side,
    loader_features, dest, block_values, row_block, col_block, w_first, b_first, w_second, b_second
):
    n = depth * side * 2
    node_dev, width = loader_features.shape
    count, block, _ = block_values.shape
    row_blocks = node_dev // block
    slots = count // n
    used = slots // row_blocks
    hidden = w_first.shape[1]
    blocks = n * row_blocks
    grid_rows = row_block.reshape(n, row_blocks, 1, used)
    hit = grid_rows == jnp.arange(row_blocks, dtype=I32)[None, None, :, None]
    number = jnp.arange(count, dtype=I32).reshape(n, row_blocks, 1, used)
    order = jnp.sum(jnp.where(hit, number, 0), axis=1).reshape(count)
    steps = 2 * depth - 1
    vmem = pl.BlockSpec(memory_space=pltpu.VMEM)
    smem = pl.BlockSpec(memory_space=pltpu.SMEM)
    dma = pltpu.SemaphoreType.DMA
    anywhere = pl.BlockSpec(memory_space=pl.ANY)
    line_sems = [dma((2, steps)), dma((steps,)), dma((2, steps)), dma((n,))]

    def params(**more):
        return pltpu.CompilerParams(vmem_limit_bytes=60 * 1024 * 1024, **more)

    table, inverse = pl.pallas_call(
        functools.partial(rows_kernel, depth, side),
        out_shape=(
            jax.ShapeDtypeStruct((n * node_dev, width), F32),
            jax.ShapeDtypeStruct((blocks, block), I32),
        ),
        in_specs=[vmem] * 2,
        out_specs=(vmem, vmem),
        scratch_shapes=[
            pltpu.VMEM((n, node_dev, width), BF16),
            pltpu.VMEM((n, row_blocks, block), I32),
            pltpu.VMEM((2 * blocks, block), F32),
            dma((n,)),
            dma((n,)),
            *line_sems,
        ],
        compiler_params=params(collective_id=0, has_side_effects=True),
    )(dest.reshape(row_blocks, block), loader_features)
    first, ordered = pl.pallas_call(
        functools.partial(first_kernel, n),
        out_shape=(
            jax.ShapeDtypeStruct((node_dev, width), BF16),
            jax.ShapeDtypeStruct(block_values.shape, BF16),
        ),
        in_specs=[smem, smem, smem, vmem, anywhere],
        out_specs=(vmem, anywhere),
        scratch_shapes=[
            pltpu.VMEM((count, block, block), BF16),
            pltpu.VMEM((n * used * block, width), F32),
            pltpu.VMEM((node_dev, width), F32),
            dma((2,)),
        ],
        compiler_params=params(),
    )(col_block, order, inverse, table, block_values)
    return pl.pallas_call(
        functools.partial(second_kernel, depth, side),
        out_shape=jax.ShapeDtypeStruct((node_dev, w_second.shape[1]), BF16),
        in_specs=[smem, vmem, anywhere] + [vmem] * 4,
        out_specs=vmem,
        scratch_shapes=[
            pltpu.VMEM((count, block, block), BF16),
            pltpu.VMEM((n, node_dev, width), BF16),
            pltpu.VMEM((node_dev, hidden), F32),
            dma(()),
            *line_sems,
        ],
        compiler_params=params(collective_id=1, has_side_effects=True),
    )(
        col_block,
        first,
        ordered,
        w_first,
        b_first.reshape(1, -1),
        w_second,
        b_second.reshape(1, -1),
    )


def solution(mesh):
    groups, wide = mesh.shape["groups"], mesh.shape["wide"]
    side = 2 if groups < 4 and wide % 4 == 0 else 1
    depth = wide // (2 * side)
    placed = (
        P(("groups", "wide"), None),
        P(("groups", "wide")),
        P(("groups", "wide"), None, None),
        P(("groups", "wide")),
        P(("groups", "wide")),
        P(),
        P(),
        P(),
        P(),
    )
    return jax.shard_map(
        functools.partial(body, depth, side),
        mesh=mesh,
        in_specs=placed,
        out_specs=P(("groups", "wide"), None),
        check_vma=False,
    )
```

```python
import functools

import jax
import jax.numpy as jnp
from jax import lax
from jax.experimental import pallas as pl
from jax.experimental.pallas import tpu as pltpu
from jax.sharding import PartitionSpec as P

MESH = pl.DeviceIdType.MESH
F32 = jnp.float32
BF16 = jnp.bfloat16
I32 = jnp.int32


def greet_all(n):
    me = lax.axis_index("wide")
    barrier = pltpu.get_barrier_semaphore()

    def greet(step, _):
        pl.semaphore_signal(
            barrier, inc=1, device_id={"wide": (me + step) % n}, device_id_type=MESH
        )
        return _

    lax.fori_loop(1, n, greet, 0)
    pl.semaphore_wait(barrier, n - 1)


def gather(depth, side, buf, own_ref, sems, extra, process):
    line_send, side_send, pair_send, recv = sems
    me = lax.axis_index("wide")
    core = me % 2
    lane_y = (me // 2) % side
    lane_z = me // (2 * side)
    pair = me + 1 - 2 * core

    def slot_of(at_z, at_y, at_core):
        return (at_z * side + at_y) * 2 + at_core

    def copy(source_ref, slot, send, target):
        return pltpu.make_async_remote_copy(
            src_ref=source_ref,
            dst_ref=buf.at[slot],
            send_sem=send,
            recv_sem=recv.at[slot],
            device_id={"wide": target},
            device_id_type=MESH,
        )

    def arrived(slot):
        copy(buf.at[slot], slot, pair_send.at[0, 0], pair).wait_recv()

    def place(d):
        off = (d + 1) // 2
        at_z = lane_z + off * (1 - 2 * (d % 2))
        valid = (d >= 0) & (at_z >= 0) & (at_z < depth)
        return at_z, valid

    right = slot_of(lane_z + 1, lane_y, core)
    left = slot_of(lane_z - 1, lane_y, core)
    across = slot_of(lane_z, 1 - lane_y, core)
    steps = 2 * depth - 1
    buf[me] = own_ref[...]

    def line_copies(d, slot):
        source = buf.at[slot]
        return (
            (copy(source, slot, line_send.at[0, d], right),
             ((d == 0) | (d % 2 == 1)) & (lane_z < depth - 1)),
            (copy(source, slot, line_send.at[1, d], left),
             (d % 2 == 0) & (lane_z > 0)),
        )

    def step(d, _):
        at_z, valid = place(d)

        @pl.when(valid & (d < steps))
        def _line():
            slot = slot_of(at_z, lane_y, core)

            @pl.when(d > 0)
            def _wait():
                arrived(slot)

            for one, go in line_copies(d, slot):
                pl.when(go)(one.start)
            if side == 2:
                copy(buf.at[slot], slot, side_send.at[d], across).start()
            copy(buf.at[slot], slot, pair_send.at[0, d], pair).start()

        extra(d)

        back_z, back_valid = place(d - 2)
        if side == 2:

            @pl.when(back_valid & (d - 2 < steps))
            def _side():
                slot = slot_of(back_z, 1 - lane_y, core)
                arrived(slot)
                copy(buf.at[slot], slot, pair_send.at[1, d - 2], pair).start()

        def kind(k, _):
            lag = jnp.where(k == 0, 0, jnp.where(k == 3, 4, 2))
            from_side = k % 2
            from_pair = k // 2
            kz, kvalid = place(d - lag)
            ky = jnp.where(from_side == 1, side - 1 - lane_y, lane_y)
            kc = jnp.where(from_pair == 1, 1 - core, core)
            slot = slot_of(kz, ky, kc)

            @pl.when(kvalid & (d - lag < steps))
            def _process():
                @pl.when(from_pair == 1)
                def _wait():
                    arrived(slot)

                process(slot)

            return _

        if side == 2:
            lax.fori_loop(0, 4, kind, 0)
        else:
            lax.fori_loop(0, 2, lambda k, c: kind(2 * k, c), 0)
        return _

    lax.fori_loop(0, steps + 4, step, 0)

    def drain(d, _):
        at_z, valid = place(d)

        @pl.when(valid)
        def _drain():
            slot = slot_of(at_z, lane_y, core)
            for one, go in line_copies(d, slot):
                pl.when(go)(one.wait_send)
            if side == 2:
                copy(buf.at[slot], slot, side_send.at[d], across).wait_send()
                other = slot_of(at_z, 1 - lane_y, core)
                copy(buf.at[other], other, pair_send.at[1, d], pair).wait_send()
            copy(buf.at[slot], slot, pair_send.at[0, d], pair).wait_send()

        return _

    lax.fori_loop(0, steps, drain, 0)


def rows_kernel(
    depth, side, dest_ref, loader_ref, table_ref, inverse_int,
    rows_buf, dest_buf, table, inverse, table_sem, dest_send, dest_recv, *sems
):
    n = depth * side * 2
    node_dev = loader_ref.shape[0]
    block = dest_ref.shape[1]
    row_blocks = node_dev // block
    me = lax.axis_index("wide")
    greet_all(n)

    def dest_copy(step, source):
        return pltpu.make_async_remote_copy(
            src_ref=dest_ref,
            dst_ref=dest_buf.at[source],
            send_sem=dest_send.at[step],
            recv_sem=dest_recv.at[source],
            device_id={"wide": (me + step) % n},
            device_id_type=MESH,
        )

    def send_dest(step, _):
        dest_copy(step, me).start()
        return _

    lax.fori_loop(1, n, send_dest, 0)
    dest_buf[me] = dest_ref[...]
    inverse[...] = jnp.zeros_like(inverse)

    blocks = n * row_blocks
    sub_hi = lax.broadcasted_iota(I32, (blocks, block), 0)
    sub_lo = lax.broadcasted_iota(I32, (block, block), 0)
    lane_hi = lax.broadcasted_iota(I32, (blocks, block), 1).astype(F32)

    def invert(source):
        @pl.when(source != me)
        def _wait():
            dest_copy(1, source).wait_recv()

        positions = dest_buf[source]
        upper, lower, right = [], [], []
        for a in range(row_blocks):
            line = positions[a : a + 1, :]
            hit = sub_hi == line // block
            number = (source * row_blocks + a).astype(F32)
            upper.append(jnp.where(hit, number, 0.0).astype(BF16))
            lower.append(jnp.where(hit, lane_hi, 0.0).astype(BF16))
            right.append(jnp.where(sub_lo == line % block, 1.0, 0.0).astype(BF16))
        left = jnp.concatenate(
            [jnp.concatenate(upper, axis=1), jnp.concatenate(lower, axis=1)], axis=0
        )
        inverse[...] += lax.dot_general(
            left,
            jnp.concatenate(right, axis=1),
            (((1,), (1,)), ((), ())),
            preferred_element_type=F32,
        )

    def invert_two(d):
        def one(k, _):
            source = 2 * d + k
            pl.when(source < n)(lambda: invert(source))
            return _

        lax.fori_loop(0, 2, one, 0)

    def table_copy(slot):
        part = pl.ds(pl.multiple_of(slot * node_dev, node_dev), node_dev)
        return pltpu.make_async_copy(table.at[part], table_ref.at[part], table_sem.at[slot])

    def widen(slot):
        start = pl.multiple_of(slot * node_dev, node_dev)
        table[pl.ds(start, node_dev), :] = rows_buf[slot].astype(F32)
        table_copy(slot).start()

    gather(depth, side, rows_buf, loader_ref, sems, invert_two, widen)

    def drain_dest(step, _):
        dest_copy(step, me).wait_send()
        return _

    lax.fori_loop(1, n, drain_dest, 0)

    def drain_table(slot, _):
        table_copy(slot).wait()
        return _

    lax.fori_loop(0, n, drain_table, 0)

    inverse_int[...] = (
        inverse[:blocks, :] * float(block) + inverse[blocks:, :]
    ).astype(I32)


def add(group, right, values, total, row_blocks):
    block = values.shape[1]
    for r in range(row_blocks):
        at = (group * row_blocks + r) * 2
        left = jnp.concatenate([values[at], values[at + 1]], axis=1)
        total[pl.ds(r * block, block), :] += jnp.dot(
            left, right, preferred_element_type=F32
        )


def first_kernel(
    n, col_ref, order_ref, inverse_ref, table_ref, values_ref, first_ref, ordered_ref,
    values, table, picked, total, local_sem
):
    load = pltpu.make_async_copy(table_ref, table, local_sem.at[2])
    load.start()

    def load_block(at, _):
        pltpu.make_async_copy(
            values_ref.at[order_ref[at]], values.at[at], local_sem.at[0]
        ).start()
        return _

    lax.fori_loop(0, values.shape[0], load_block, 0, unroll=8)
    block = values.shape[1]
    row_blocks = first_ref.shape[0] // block
    slots = values.shape[0] // n

    def pick(t, _):
        column = col_ref[(t // 2) * slots + t % 2]

        def fetch(j, _):
            rows = [inverse_ref[column, j * 32 + k] for k in range(32)]
            rows = [table[pl.ds(row, 1), :] for row in rows]
            for k, row in enumerate(rows):
                picked[pl.ds(t * block + j * 32 + k, 1), :] = row
            return _

        return lax.fori_loop(0, block // 32, fetch, _)

    load.wait()
    lax.fori_loop(0, 2 * n, pick, 0)
    pltpu.make_async_copy(values_ref, values, local_sem.at[0]).wait()
    store = pltpu.make_async_copy(values, ordered_ref, local_sem.at[1])
    store.start()
    total[...] = jnp.zeros_like(total)

    def group_step(group, _):
        start = pl.multiple_of(group * 2 * block, 2 * block)
        right = picked[pl.ds(start, 2 * block), :].astype(BF16)
        add(group, right, values, total, row_blocks)
        return _

    lax.fori_loop(0, n, group_step, 0)
    first_ref[...] = total[...].astype(BF16)
    store.wait()


def second_kernel(
    depth, side, col_ref, first_ref, values_ref,
    w_first_ref, b_first_ref, w_second_ref, b_second_ref, out_ref,
    values, first_buf, total, local_sem, *sems
):
    n = depth * side * 2
    load = pltpu.make_async_copy(values_ref, values, local_sem)
    load.start()
    block = values.shape[1]
    row_blocks = first_ref.shape[0] // block
    slots = values.shape[0] // n
    greet_all(n)
    total[...] = jnp.zeros_like(total)
    load.wait()

    def second_group(slot):
        tiles = []
        for u in range(2):
            column = col_ref[slot * slots + u] - slot * row_blocks
            tile = first_buf[slot, :block]
            for b in range(1, row_blocks):
                tile = jnp.where(
                    column == b, first_buf[slot, b * block : (b + 1) * block], tile
                )
            tiles.append(tile)
        tiles = jnp.concatenate(tiles, axis=0)
        hidden = jnp.dot(tiles, w_first_ref[...], preferred_element_type=F32)
        hidden = jnp.maximum(hidden + b_first_ref[...], 0.0).astype(BF16)
        add(slot, hidden, values, total, row_blocks)

    gather(depth, side, first_buf, first_ref, sems, lambda d: None, second_group)
    out_ref[...] = (
        jnp.dot(total[...].astype(BF16), w_second_ref[...], preferred_element_type=F32)
        + b_second_ref[...]
    ).astype(BF16)


def body(
    depth, side,
    loader_features, dest, block_values, row_block, col_block, w_first, b_first, w_second, b_second
):
    n = depth * side * 2
    node_dev, width = loader_features.shape
    count, block, _ = block_values.shape
    row_blocks = node_dev // block
    slots = count // n
    used = slots // row_blocks
    hidden = w_first.shape[1]
    blocks = n * row_blocks
    grid_rows = row_block.reshape(n, row_blocks, 1, used)
    hit = grid_rows == jnp.arange(row_blocks, dtype=I32)[None, None, :, None]
    number = jnp.arange(count, dtype=I32).reshape(n, row_blocks, 1, used)
    order = jnp.sum(jnp.where(hit, number, 0), axis=1).reshape(count)
    steps = 2 * depth - 1
    vmem = pl.BlockSpec(memory_space=pltpu.VMEM)
    smem = pl.BlockSpec(memory_space=pltpu.SMEM)
    dma = pltpu.SemaphoreType.DMA
    anywhere = pl.BlockSpec(memory_space=pl.ANY)
    line_sems = [dma((2, steps)), dma((steps,)), dma((2, steps)), dma((n,))]

    def params(**more):
        return pltpu.CompilerParams(vmem_limit_bytes=60 * 1024 * 1024, **more)

    table, inverse = pl.pallas_call(
        functools.partial(rows_kernel, depth, side),
        out_shape=(
            jax.ShapeDtypeStruct((n * node_dev, width), F32),
            jax.ShapeDtypeStruct((blocks, block), I32),
        ),
        in_specs=[vmem] * 2,
        out_specs=(anywhere, vmem),
        scratch_shapes=[
            pltpu.VMEM((n, node_dev, width), BF16),
            pltpu.VMEM((n, row_blocks, block), I32),
            pltpu.VMEM((n * node_dev, width), F32),
            pltpu.VMEM((2 * blocks, block), F32),
            dma((n,)),
            dma((n,)),
            dma((n,)),
            *line_sems,
        ],
        compiler_params=params(collective_id=0, has_side_effects=True),
    )(dest.reshape(row_blocks, block), loader_features)
    first, ordered = pl.pallas_call(
        functools.partial(first_kernel, n),
        out_shape=(
            jax.ShapeDtypeStruct((node_dev, width), BF16),
            jax.ShapeDtypeStruct(block_values.shape, BF16),
        ),
        in_specs=[smem, smem, smem, anywhere, anywhere],
        out_specs=(vmem, anywhere),
        scratch_shapes=[
            pltpu.VMEM((count, block, block), BF16),
            pltpu.VMEM((n * node_dev, width), F32),
            pltpu.VMEM((n * used * block, width), F32),
            pltpu.VMEM((node_dev, width), F32),
            dma((3,)),
        ],
        compiler_params=params(),
    )(col_block, order, inverse, table, block_values)
    return pl.pallas_call(
        functools.partial(second_kernel, depth, side),
        out_shape=jax.ShapeDtypeStruct((node_dev, w_second.shape[1]), BF16),
        in_specs=[smem, vmem, anywhere] + [vmem] * 4,
        out_specs=vmem,
        scratch_shapes=[
            pltpu.VMEM((count, block, block), BF16),
            pltpu.VMEM((n, node_dev, width), BF16),
            pltpu.VMEM((node_dev, hidden), F32),
            dma(()),
            *line_sems,
        ],
        compiler_params=params(collective_id=1, has_side_effects=True),
    )(
        col_block,
        first,
        ordered,
        w_first,
        b_first.reshape(1, -1),
        w_second,
        b_second.reshape(1, -1),
    )


def solution(mesh):
    groups, wide = mesh.shape["groups"], mesh.shape["wide"]
    side = 2 if groups < 4 and wide % 4 == 0 else 1
    depth = wide // (2 * side)
    placed = (
        P(("groups", "wide"), None),
        P(("groups", "wide")),
        P(("groups", "wide"), None, None),
        P(("groups", "wide")),
        P(("groups", "wide")),
        P(),
        P(),
        P(),
        P(),
    )
    return jax.shard_map(
        functools.partial(body, depth, side),
        mesh=mesh,
        in_specs=placed,
        out_specs=P(("groups", "wide"), None),
        check_vma=False,
    )
```

```python
import functools

import jax
import jax.numpy as jnp
from jax import lax
from jax.experimental import pallas as pl
from jax.experimental.pallas import tpu as pltpu
from jax.sharding import PartitionSpec as P

MESH = pl.DeviceIdType.MESH
F32 = jnp.float32
BF16 = jnp.bfloat16
I32 = jnp.int32


def greet_all(n):
    me = lax.axis_index("wide")
    barrier = pltpu.get_barrier_semaphore()

    def greet(step, _):
        pl.semaphore_signal(
            barrier, inc=1, device_id={"wide": (me + step) % n}, device_id_type=MESH
        )
        return _

    lax.fori_loop(1, n, greet, 0)
    pl.semaphore_wait(barrier, n - 1)


def gather(depth, side, buf, own_ref, sems, extra, process):
    line_send, side_send, pair_send, recv = sems
    me = lax.axis_index("wide")
    core = me % 2
    lane_y = (me // 2) % side
    lane_z = me // (2 * side)
    pair = me + 1 - 2 * core

    def slot_of(at_z, at_y, at_core):
        return (at_z * side + at_y) * 2 + at_core

    rows = buf.shape[1]
    cut = rows * 3 // 4
    parts = (pl.ds(0, cut), pl.ds(cut, rows - cut))

    def copy(slot, part, send, target):
        return pltpu.make_async_remote_copy(
            src_ref=buf.at[slot, parts[part]],
            dst_ref=buf.at[slot, parts[part]],
            send_sem=send,
            recv_sem=recv.at[part, slot],
            device_id={"wide": target},
            device_id_type=MESH,
        )

    def arrived(slot, part):
        copy(slot, part, pair_send.at[0, 0], pair).wait_recv()

    def place(d):
        off = (d + 1) // 2
        at_z = lane_z + off * (1 - 2 * (d % 2))
        valid = (d >= 0) & (at_z >= 0) & (at_z < depth)
        return at_z, valid

    right = slot_of(lane_z + 1, lane_y, core)
    left = slot_of(lane_z - 1, lane_y, core)
    across = slot_of(lane_z, 1 - lane_y, core)
    steps = 2 * depth - 1
    buf[me] = own_ref[...]

    kinds = (1, 0, 2) if side == 2 else (1, 0)

    def kind_of(q, at_z):
        at_y = 1 - lane_y if q == 2 else lane_y
        return slot_of(at_z, at_y, core), min(q, 1)

    def line_copies(d, q, slot, part):
        return (
            (copy(slot, part, line_send.at[0, q, d], right),
             ((d == 0) | (d % 2 == 1)) & (lane_z < depth - 1)),
            (copy(slot, part, line_send.at[1, q, d], left),
             (d % 2 == 0) & (lane_z > 0)),
        )

    def step(d, _):
        at_z, valid = place(d)

        @pl.when(valid & (d < steps))
        def _line():
            for q in kinds:
                slot, part = kind_of(q, at_z)
                if q == 2:
                    arrived(slot, part)
                else:
                    pl.when(d > 0)(functools.partial(arrived, slot, part))
                if side == 2 and q == 1:
                    pl.when(d == 0)(
                        copy(slot, part, side_send.at[steps], across).start
                    )
                for one, go in line_copies(d, q, slot, part):
                    pl.when(go)(one.start)
                if side == 2 and q == 0:
                    copy(slot, part, side_send.at[d], across).start()
                copy(slot, part, pair_send.at[q, d], pair).start()

        extra(d)

        back_z, back_valid = place(d - 2)
        if side == 2:

            @pl.when(back_valid & (d - 2 < steps))
            def _side():
                slot = slot_of(back_z, 1 - lane_y, core)
                arrived(slot, 0)
                copy(slot, 0, pair_send.at[3, d - 2], pair).start()

        def kind(k, _):
            lag = jnp.where(k == 0, 0, jnp.where(k == 3, 4, 2))
            from_side = k % 2
            from_pair = k // 2
            kz, kvalid = place(d - lag)
            ky = jnp.where(from_side == 1, side - 1 - lane_y, lane_y)
            kc = jnp.where(from_pair == 1, 1 - core, core)
            slot = slot_of(kz, ky, kc)

            @pl.when(kvalid & (d - lag < steps))
            def _process():
                @pl.when(from_pair == 1)
                def _wait():
                    arrived(slot, 0)
                    arrived(slot, 1)

                process(slot)

            return _

        if side == 2:
            lax.fori_loop(0, 4, kind, 0)
        else:
            lax.fori_loop(0, 2, lambda k, c: kind(2 * k, c), 0)
        return _

    lax.fori_loop(0, steps + 4, step, 0)

    def drain(d, _):
        at_z, valid = place(d)

        @pl.when(valid)
        def _drain():
            for q in kinds:
                slot, part = kind_of(q, at_z)
                for one, go in line_copies(d, q, slot, part):
                    pl.when(go)(one.wait_send)
                copy(slot, part, pair_send.at[q, d], pair).wait_send()
                if side == 2 and q == 1:
                    pl.when(d == 0)(
                        copy(slot, part, side_send.at[steps], across).wait_send
                    )
                if side == 2 and q == 0:
                    copy(slot, part, side_send.at[d], across).wait_send()
            if side == 2:
                other = slot_of(at_z, 1 - lane_y, core)
                copy(other, 0, pair_send.at[3, d], pair).wait_send()

        return _

    lax.fori_loop(0, steps, drain, 0)


def rows_kernel(
    depth, side, dest_ref, loader_ref, table_ref, inverse_int,
    rows_buf, dest_buf, table, inverse, table_sem, dest_send, dest_recv, *sems
):
    n = depth * side * 2
    node_dev = loader_ref.shape[0]
    block = dest_ref.shape[1]
    row_blocks = node_dev // block
    me = lax.axis_index("wide")
    greet_all(n)

    def dest_copy(step, source):
        return pltpu.make_async_remote_copy(
            src_ref=dest_ref,
            dst_ref=dest_buf.at[source],
            send_sem=dest_send.at[step],
            recv_sem=dest_recv.at[source],
            device_id={"wide": (me + step) % n},
            device_id_type=MESH,
        )

    def send_dest(step, _):
        dest_copy(step, me).start()
        return _

    lax.fori_loop(1, n, send_dest, 0)
    dest_buf[me] = dest_ref[...]
    inverse[...] = jnp.zeros_like(inverse)

    blocks = n * row_blocks
    sub_hi = lax.broadcasted_iota(I32, (blocks, block), 0)
    sub_lo = lax.broadcasted_iota(I32, (block, block), 0)
    lane_hi = lax.broadcasted_iota(I32, (blocks, block), 1).astype(F32)

    def invert(source):
        @pl.when(source != me)
        def _wait():
            dest_copy(1, source).wait_recv()

        positions = dest_buf[source]
        upper, lower, right = [], [], []
        for a in range(row_blocks):
            line = positions[a : a + 1, :]
            hit = sub_hi == line // block
            number = (source * row_blocks + a).astype(F32)
            upper.append(jnp.where(hit, number, 0.0).astype(BF16))
            lower.append(jnp.where(hit, lane_hi, 0.0).astype(BF16))
            right.append(jnp.where(sub_lo == line % block, 1.0, 0.0).astype(BF16))
        left = jnp.concatenate(
            [jnp.concatenate(upper, axis=1), jnp.concatenate(lower, axis=1)], axis=0
        )
        inverse[...] += lax.dot_general(
            left,
            jnp.concatenate(right, axis=1),
            (((1,), (1,)), ((), ())),
            preferred_element_type=F32,
        )

    def invert_two(d):
        def one(k, _):
            source = 2 * d + k
            pl.when(source < n)(lambda: invert(source))
            return _

        lax.fori_loop(0, 2, one, 0)

    def table_copy(slot):
        part = pl.ds(pl.multiple_of(slot * node_dev, node_dev), node_dev)
        return pltpu.make_async_copy(table.at[part], table_ref.at[part], table_sem.at[slot])

    def widen(slot):
        start = pl.multiple_of(slot * node_dev, node_dev)
        table[pl.ds(start, node_dev), :] = rows_buf[slot].astype(F32)
        table_copy(slot).start()

    gather(depth, side, rows_buf, loader_ref, sems, invert_two, widen)

    def drain_dest(step, _):
        dest_copy(step, me).wait_send()
        return _

    lax.fori_loop(1, n, drain_dest, 0)

    def drain_table(slot, _):
        table_copy(slot).wait()
        return _

    lax.fori_loop(0, n, drain_table, 0)

    inverse_int[...] = (
        inverse[:blocks, :] * float(block) + inverse[blocks:, :]
    ).astype(I32)


def add(group, right, values, total, row_blocks):
    block = values.shape[1]
    for r in range(row_blocks):
        at = (group * row_blocks + r) * 2
        left = jnp.concatenate([values[at], values[at + 1]], axis=1)
        total[pl.ds(r * block, block), :] += jnp.dot(
            left, right, preferred_element_type=F32
        )


def first_kernel(
    n, col_ref, order_ref, inverse_ref, table_ref, values_ref, first_ref, ordered_ref,
    values, table, picked, total, local_sem
):
    load = pltpu.make_async_copy(table_ref, table, local_sem.at[2])
    load.start()

    def load_block(at, _):
        pltpu.make_async_copy(
            values_ref.at[order_ref[at]], values.at[at], local_sem.at[0]
        ).start()
        return _

    lax.fori_loop(0, values.shape[0], load_block, 0, unroll=8)
    block = values.shape[1]
    row_blocks = first_ref.shape[0] // block
    slots = values.shape[0] // n

    def pick(t, _):
        column = col_ref[(t // 2) * slots + t % 2]

        def fetch(j, _):
            rows = [inverse_ref[column, j * 32 + k] for k in range(32)]
            rows = [table[pl.ds(row, 1), :] for row in rows]
            for k, row in enumerate(rows):
                picked[pl.ds(t * block + j * 32 + k, 1), :] = row
            return _

        return lax.fori_loop(0, block // 32, fetch, _)

    load.wait()
    lax.fori_loop(0, 2 * n, pick, 0)
    pltpu.make_async_copy(values_ref, values, local_sem.at[0]).wait()
    store = pltpu.make_async_copy(values, ordered_ref, local_sem.at[1])
    store.start()
    total[...] = jnp.zeros_like(total)

    def group_step(group, _):
        start = pl.multiple_of(group * 2 * block, 2 * block)
        right = picked[pl.ds(start, 2 * block), :].astype(BF16)
        add(group, right, values, total, row_blocks)
        return _

    lax.fori_loop(0, n, group_step, 0)
    first_ref[...] = total[...].astype(BF16)
    store.wait()


def second_kernel(
    depth, side, col_ref, first_ref, values_ref,
    w_first_ref, b_first_ref, w_second_ref, b_second_ref, out_ref,
    values, first_buf, total, local_sem, *sems
):
    n = depth * side * 2
    load = pltpu.make_async_copy(values_ref, values, local_sem)
    load.start()
    block = values.shape[1]
    row_blocks = first_ref.shape[0] // block
    slots = values.shape[0] // n
    greet_all(n)
    total[...] = jnp.zeros_like(total)
    load.wait()

    def second_group(slot):
        tiles = []
        for u in range(2):
            column = col_ref[slot * slots + u] - slot * row_blocks
            tile = first_buf[slot, :block]
            for b in range(1, row_blocks):
                tile = jnp.where(
                    column == b, first_buf[slot, b * block : (b + 1) * block], tile
                )
            tiles.append(tile)
        tiles = jnp.concatenate(tiles, axis=0)
        hidden = jnp.dot(tiles, w_first_ref[...], preferred_element_type=F32)
        hidden = jnp.maximum(hidden + b_first_ref[...], 0.0).astype(BF16)
        add(slot, hidden, values, total, row_blocks)

    gather(depth, side, first_buf, first_ref, sems, lambda d: None, second_group)
    out_ref[...] = (
        jnp.dot(total[...].astype(BF16), w_second_ref[...], preferred_element_type=F32)
        + b_second_ref[...]
    ).astype(BF16)


def body(
    depth, side,
    loader_features, dest, block_values, row_block, col_block, w_first, b_first, w_second, b_second
):
    n = depth * side * 2
    node_dev, width = loader_features.shape
    count, block, _ = block_values.shape
    row_blocks = node_dev // block
    slots = count // n
    used = slots // row_blocks
    hidden = w_first.shape[1]
    blocks = n * row_blocks
    grid_rows = row_block.reshape(n, row_blocks, 1, used)
    hit = grid_rows == jnp.arange(row_blocks, dtype=I32)[None, None, :, None]
    number = jnp.arange(count, dtype=I32).reshape(n, row_blocks, 1, used)
    order = jnp.sum(jnp.where(hit, number, 0), axis=1).reshape(count)
    steps = 2 * depth - 1
    vmem = pl.BlockSpec(memory_space=pltpu.VMEM)
    smem = pl.BlockSpec(memory_space=pltpu.SMEM)
    dma = pltpu.SemaphoreType.DMA
    anywhere = pl.BlockSpec(memory_space=pl.ANY)
    line_sems = [dma((2, 3, steps)), dma((steps + 1,)), dma((4, steps)), dma((2, n))]

    def params(**more):
        return pltpu.CompilerParams(vmem_limit_bytes=60 * 1024 * 1024, **more)

    table, inverse = pl.pallas_call(
        functools.partial(rows_kernel, depth, side),
        out_shape=(
            jax.ShapeDtypeStruct((n * node_dev, width), F32),
            jax.ShapeDtypeStruct((blocks, block), I32),
        ),
        in_specs=[vmem] * 2,
        out_specs=(anywhere, vmem),
        scratch_shapes=[
            pltpu.VMEM((n, node_dev, width), BF16),
            pltpu.VMEM((n, row_blocks, block), I32),
            pltpu.VMEM((n * node_dev, width), F32),
            pltpu.VMEM((2 * blocks, block), F32),
            dma((n,)),
            dma((n,)),
            dma((n,)),
            *line_sems,
        ],
        compiler_params=params(collective_id=0, has_side_effects=True),
    )(dest.reshape(row_blocks, block), loader_features)
    first, ordered = pl.pallas_call(
        functools.partial(first_kernel, n),
        out_shape=(
            jax.ShapeDtypeStruct((node_dev, width), BF16),
            jax.ShapeDtypeStruct(block_values.shape, BF16),
        ),
        in_specs=[smem, smem, smem, anywhere, anywhere],
        out_specs=(vmem, anywhere),
        scratch_shapes=[
            pltpu.VMEM((count, block, block), BF16),
            pltpu.VMEM((n * node_dev, width), F32),
            pltpu.VMEM((n * used * block, width), F32),
            pltpu.VMEM((node_dev, width), F32),
            dma((3,)),
        ],
        compiler_params=params(),
    )(col_block, order, inverse, table, block_values)
    return pl.pallas_call(
        functools.partial(second_kernel, depth, side),
        out_shape=jax.ShapeDtypeStruct((node_dev, w_second.shape[1]), BF16),
        in_specs=[smem, vmem, anywhere] + [vmem] * 4,
        out_specs=vmem,
        scratch_shapes=[
            pltpu.VMEM((count, block, block), BF16),
            pltpu.VMEM((n, node_dev, width), BF16),
            pltpu.VMEM((node_dev, hidden), F32),
            dma(()),
            *line_sems,
        ],
        compiler_params=params(collective_id=1, has_side_effects=True),
    )(
        col_block,
        first,
        ordered,
        w_first,
        b_first.reshape(1, -1),
        w_second,
        b_second.reshape(1, -1),
    )


def solution(mesh):
    groups, wide = mesh.shape["groups"], mesh.shape["wide"]
    side = 2 if groups < 4 and wide % 4 == 0 else 1
    depth = wide // (2 * side)
    placed = (
        P(("groups", "wide"), None),
        P(("groups", "wide")),
        P(("groups", "wide"), None, None),
        P(("groups", "wide")),
        P(("groups", "wide")),
        P(),
        P(),
        P(),
        P(),
    )
    return jax.shard_map(
        functools.partial(body, depth, side),
        mesh=mesh,
        in_specs=placed,
        out_specs=P(("groups", "wide"), None),
        check_vma=False,
    )
```
